32 devices in a mesh: space: 8 (over z, x), inst: 4 (over y, core).
Axes of the slice: x: 2, y: 2, z: 4, core: 2. Of those that a mesh axis runs over, the one named last changes fastest.
Arguments:
- basis_rows: bfloat16 [2, 24576, 512], P(None, 'space'), may hold values from -0.75 to 0.75
- reference_state: float32 [2, 24576], P(None, 'space'), may hold values from -3 to 3
- burning: int32 [24576], P('space'), may hold values 0 or 1
- coords_now: float32 [4, 512], P('inst'), may hold values from -1.5 to 1.5
- coords_before: float32 [4, 512], P('inst'), may hold values from -1.5 to 1.5
- diffusivity: float32 [4], P('inst'), may hold values from 0.5 to 2
- advection: float32 [4], P('inst'), may hold values from 0.5 to 1.5
- reaction_rate: float32 [4], P('inst'), may hold values from 0.2 to 1
Outputs:
- jacobian: bfloat16 [4, 2, 24576, 512], P('inst', None, 'space')
- residual: float32 [4, 2, 24576], P('inst', None, 'space')
- update: float32 [4, 512], P('inst')
The draws below stay inside these ranges and needn't reach their ends.
All inputs are finite; a program needn't handle non-finite values. No bound on the sum of `burning` on one device may be relied on, other than what follows from the above.
Results may differ from the reference program's by a relative error of at most 0.0034.
Values may be sent and summed in bfloat16 or wider, within the bound.
A program may use at most 128 MiB of HBM per device.

```python
import math
import jax
import jax.numpy as jnp
from jax import lax

MODES = 512
CELLS_DEV = 3072
INST = 4
CELLS = 24576
N_SPACE = 8


def draw_basis_rows(key, part):
    key = jax.random.fold_in(key, 11)
    partner_one = jax.random.permutation(jax.random.fold_in(key, 1), MODES)
    partner_two = jax.random.permutation(jax.random.fold_in(key, 2), MODES)
    partner_three = jax.random.permutation(jax.random.fold_in(key, 3), MODES)
    weights = jax.random.uniform(jax.random.fold_in(key, 5), (3, MODES), jnp.float32, 0.25, 0.32)
    mode_scale = jnp.exp(jax.random.uniform(jax.random.fold_in(key, 6), (MODES,), jnp.float32, math.log(0.5), math.log(1.5)))

    def one_variable(index):
        subkey = jax.random.fold_in(key, 100 + index)
        fields = 0.1 * jnp.clip(jax.random.normal(subkey, (CELLS, MODES), jnp.float32), -2.5, 2.5)
        mixed = fields + weights[0] * jnp.take(fields, partner_one, axis=1)
        mixed = mixed + weights[1] * jnp.take(fields, partner_two, axis=1)
        mixed = mixed + weights[2] * jnp.take(fields, partner_three, axis=1)
        return (mixed * mode_scale).astype(jnp.bfloat16)
    return lax.map(one_variable, jnp.arange(2, dtype=jnp.int32))


def with_ends(drawn, stream_key, low, largest):
    shape = drawn.shape
    spot = [jax.random.randint(jax.random.fold_in(stream_key, axis), (), 0, shape[axis]) for axis in range(len(shape))]
    drawn = drawn.at[tuple(spot)].set(low)
    longest = shape.index(max(shape))
    spot[longest] = (spot[longest] + 1) % shape[longest]
    return drawn.at[tuple(spot)].set(largest)


def steps_of(rng, dims, shards, smallest, top_value):
    factor_of, own = 1.0, jax.random.fold_in(rng, 6)
    for dim, shards_of in shards:
        draws = jnp.exp(jax.random.uniform(jax.random.fold_in(own, dim), (shards_of,), jnp.float32, smallest / len(shards), top_value / len(shards)))
        factor_of = factor_of * jnp.repeat(draws, dims[dim] // shards_of).reshape([-1 if axis == dim else 1 for axis in range(len(dims))])
    return factor_of


def normal_values(own_key, extent, deviation, most, pieces=(), kind=jnp.bfloat16):
    loudness = steps_of(own_key, extent, pieces, -0.22, 0.18) if pieces else 1.0
    result = jax.random.normal(own_key, extent, jnp.float32) * deviation * loudness
    return jnp.minimum(jnp.maximum(result, -most), most).astype(kind)


def setup_inputs(seed: int = 0) -> dict:
    key_list = jax.random.split(jax.random.key(seed), 9)
    basis_rows = draw_basis_rows(jax.random.fold_in(key_list[8], 71), 0)
    reference_state = normal_values(key_list[1], (2, CELLS), 0.5, 3.0, ((1, 8),), jnp.float32)
    burning = with_ends((jax.random.randint(key_list[2], (CELLS,), 0, 2) < 1).astype(jnp.int32), jax.random.fold_in(key_list[2], 1), 0, 1)
    coords_now = normal_values(key_list[3], (INST, MODES), 0.25, 1.5, ((0, 4),), jnp.float32)
    coords_before = normal_values(key_list[4], (INST, MODES), 0.25, 1.5, ((0, 4),), jnp.float32)
    diffusivity = jnp.clip(jnp.exp(math.log(2.0) - 1.3862944 * jax.random.uniform(key_list[5], (INST,), jnp.float32) ** steps_of(key_list[5], (INST,), ((0, 4),), -0.2, 0.2)), 0.5, 2.0)
    advection = jnp.clip(0.5 + 1.0 * jax.random.uniform(key_list[6], (INST,), jnp.float32) ** steps_of(key_list[6], (INST,), ((0, 4),), -0.2, 0.2), 0.5, 1.5)
    reaction_rate = jnp.clip(jnp.exp(math.log(1.0) - 1.609438 * jax.random.uniform(key_list[7], (INST,), jnp.float32) ** steps_of(key_list[7], (INST,), ((0, 4),), -0.2, 0.2)), 0.2, 1.0)
    return dict(basis_rows=basis_rows, reference_state=reference_state, burning=burning, coords_now=coords_now, coords_before=coords_before, diffusivity=diffusivity, advection=advection, reaction_rate=reaction_rate)


time_step = 0.5

def operate(padded, diffuse, advect):
    centre = padded[:, 1:-1]
    left_side = padded[:, :-2]
    right_side = padded[:, 2:]
    return diffuse * (left_side - 2.0 * centre + right_side) - advect * (centre - left_side)

def jacobian_rows(basis_piece, fuel_slope, heat_slope, diffuse, advect):
    widened = basis_piece.astype(jnp.float32)
    centre = widened[:, 1:-1]
    transport = operate(widened, diffuse, advect)
    fuel_col = centre[0] - time_step * (transport[0] - fuel_slope[:, None] * centre[0] - heat_slope[:, None] * centre[1])
    heat_col = centre[1] - time_step * (transport[1] + fuel_slope[:, None] * centre[0] + heat_slope[:, None] * centre[1])
    return jnp.stack([fuel_col, heat_col]).astype(jnp.bfloat16)

def solve_update(system, right_hand):
    factor_low = jnp.linalg.cholesky(system)
    half_solved = lax.linalg.triangular_solve(factor_low, right_hand[:, None], left_side=True, lower=True)
    solved = lax.linalg.triangular_solve(factor_low, half_solved, left_side=True, lower=True, transpose_a=True)
    return -solved[:, 0]

def one_instance(basis_rows, reference_state, burning, coords_now, coords_before, diffuse, advect, rate):
    cell_total = basis_rows.shape[1]
    mode_total = basis_rows.shape[2]
    matrix = basis_rows.reshape(2 * cell_total, mode_total)
    state_now = reference_state + jnp.dot(matrix.astype(jnp.float32), coords_now.astype(jnp.bfloat16).astype(jnp.float32), preferred_element_type=jnp.float32).reshape(2, cell_total)
    change = jnp.dot(matrix.astype(jnp.float32), (coords_now - coords_before).astype(jnp.bfloat16).astype(jnp.float32), preferred_element_type=jnp.float32).reshape(2, cell_total)
    padded_state = jnp.pad(state_now, ((0, 0), (1, 1)))
    flux_sum = operate(padded_state, diffuse, advect)
    fuel_part = state_now[0]
    heat_part = state_now[1]
    active = burning.astype(jnp.float32)
    tangent = jnp.tanh(heat_part)
    reaction = rate * active * fuel_part * (1.0 + tangent)
    residual = change - time_step * (flux_sum + jnp.stack([-reaction, reaction]))
    fuel_slope = rate * active * (1.0 + tangent)
    heat_slope = rate * active * fuel_part * (1.0 - tangent * tangent)
    padded_basis = jnp.pad(basis_rows, ((0, 0), (1, 1), (0, 0)))

    def block_rows(block_id):
        start = (block_id * CELLS_DEV).astype(jnp.int32)
        basis_piece = lax.dynamic_slice_in_dim(padded_basis, start, CELLS_DEV + 2, 1)
        fuel_block = lax.dynamic_slice_in_dim(fuel_slope, start, CELLS_DEV, 0)
        heat_block = lax.dynamic_slice_in_dim(heat_slope, start, CELLS_DEV, 0)
        return jacobian_rows(basis_piece, fuel_block, heat_block, diffuse, advect)
    stacked = lax.map(block_rows, jnp.arange(N_SPACE, dtype=jnp.int32))
    jacobian = stacked.transpose(1, 0, 2, 3).reshape(2, cell_total, mode_total)
    flat_jac = jacobian.reshape(2 * cell_total, mode_total)
    system = lax.dot_general(flat_jac.astype(jnp.float32), flat_jac.astype(jnp.float32), (((0,), (0,)), ((), ())), preferred_element_type=jnp.float32)
    right_hand = lax.dot_general(flat_jac.astype(jnp.float32), residual.astype(jnp.bfloat16).reshape(2 * cell_total).astype(jnp.float32), (((0,), (0,)), ((), ())), preferred_element_type=jnp.float32)
    return (jacobian, residual, solve_update(system, right_hand))

def reference(basis_rows, reference_state, burning, coords_now, coords_before, diffusivity, advection, reaction_rate):
    jac_list = []
    res_list = []
    upd_list = []
    for instance in range(INST):
        jacobian, residual, update = one_instance(basis_rows, reference_state, burning, coords_now[instance], coords_before[instance], diffusivity[instance], advection[instance], reaction_rate[instance])
        jac_list.append(jacobian)
        res_list.append(residual)
        upd_list.append(update)
    return (jnp.stack(jac_list), jnp.stack(res_list), jnp.stack(upd_list))
```

```python
import functools

import jax
import jax.numpy as jnp
from jax import lax
from jax.experimental import pallas as pl
from jax.experimental.pallas import tpu as pltpu
from jax.sharding import PartitionSpec as P

time_step = 0.5
MESH = pl.DeviceIdType.MESH
TILE = 512
ROWS = 32
LANES = 128
EDGE = 16
HIGH = lax.Precision.HIGHEST


def tn_dot(a, b, precision=None):
    return lax.dot_general(
        a, b, (((0,), (0,)), ((), ())), preferred_element_type=jnp.float32, precision=precision
    )


def nt_dot(a, b, precision=None):
    return lax.dot_general(
        a, b, (((1,), (1,)), ((), ())), preferred_element_type=jnp.float32, precision=precision
    )


def halo_kernel(n, basis, ref, low_b, high_b, low_r, high_r, send, recv):
    me = lax.axis_index("space")
    cells = basis.shape[1]
    has_low, has_high = me > 0, me < n - 1

    low_b[...] = jnp.zeros_like(low_b)
    high_b[...] = jnp.zeros_like(high_b)
    low_r[...] = jnp.zeros_like(low_r)
    high_r[...] = jnp.zeros_like(high_r)

    barrier = pltpu.get_barrier_semaphore()
    for step in (1, n - 1):
        pl.semaphore_signal(
            barrier, inc=1, device_id={"space": lax.rem(me + step, n)}, device_id_type=MESH
        )
    pl.semaphore_wait(barrier, 2)

    up = {"space": lax.rem(me + 1, n)}
    down = {"space": lax.rem(me + n - 1, n)}

    def copy(src, dst, slot, target):
        return pltpu.make_async_remote_copy(
            src_ref=src,
            dst_ref=dst,
            send_sem=send.at[slot],
            recv_sem=recv.at[slot],
            device_id=target,
            device_id_type=MESH,
        )

    to_up = [
        copy(basis.at[:, pl.ds(cells - EDGE, EDGE), :], low_b, 0, up),
        copy(ref.at[:, pl.ds(cells - LANES, LANES)], low_r, 1, up),
    ]
    to_down = [
        copy(basis.at[:, pl.ds(0, EDGE), :], high_b, 2, down),
        copy(ref.at[:, pl.ds(0, LANES)], high_r, 3, down),
    ]

    @pl.when(has_high)
    def _():
        for c in to_up:
            c.start()

    @pl.when(has_low)
    def _():
        for c in to_down:
            c.start()

    @pl.when(has_high)
    def _():
        for c in to_up:
            c.wait_send()
        for c in to_down:
            c.wait_recv()

    @pl.when(has_low)
    def _():
        for c in to_down:
            c.wait_send()
        for c in to_up:
            c.wait_recv()


def halo(n, basis, ref):
    modes = basis.shape[2]
    vmem = pl.BlockSpec(memory_space=pltpu.VMEM)
    return pl.pallas_call(
        functools.partial(halo_kernel, n),
        out_shape=[
            jax.ShapeDtypeStruct((2, EDGE, modes), jnp.bfloat16),
            jax.ShapeDtypeStruct((2, EDGE, modes), jnp.bfloat16),
            jax.ShapeDtypeStruct((2, LANES), jnp.float32),
            jax.ShapeDtypeStruct((2, LANES), jnp.float32),
        ],
        in_specs=[pl.BlockSpec(memory_space=pl.ANY)] * 2,
        out_specs=[vmem] * 4,
        scratch_shapes=[pltpu.SemaphoreType.DMA((4,)), pltpu.SemaphoreType.DMA((4,))],
        compiler_params=pltpu.CompilerParams(collective_id=0, has_side_effects=True),
    )(basis, ref)


def main_kernel(
    diffusivity, advection, rate, now_ref, before_ref, ref_ref, burn_ref, basis, before_rows,
    after_rows, low_b, high_b, low_r, high_r,
    jac, res_out, packed,
    state, coef, resid, wide, top, bottom, right,
):
    phase, tile = pl.program_id(0), pl.program_id(1)
    tiles = pl.num_programs(1)
    cells = res_out.shape[1]
    modes = basis.shape[2]
    half = modes // 2
    here = pl.ds(pl.multiple_of(tile * TILE, TILE), TILE)
    inner = pl.ds(pl.multiple_of(tile * TILE + LANES, LANES), TILE)
    h = time_step
    nu, c, k = diffusivity[0], advection[0], rate[0]

    def coords():
        now, old = now_ref[...], before_ref[...]
        row = lax.broadcasted_iota(jnp.int32, (16, modes), 0)
        both = jnp.where(row == 0, now, jnp.where(row == 1, now - old, 0.0))
        return both.astype(jnp.bfloat16)

    @pl.when(phase == 0)
    def _():
        vec = coords()

        @pl.when(tile == 0)
        def _():
            state[...] = jnp.zeros_like(state)
            resid[...] = jnp.zeros_like(resid)
            lane = lax.broadcasted_iota(jnp.int32, (1, LANES), 1)
            for v in range(2):
                low = nt_dot(vec, low_b[v])[0:1, EDGE - 1 : EDGE]
                state[v : v + 1, 0:LANES] = jnp.where(
                    lane == LANES - 1, low_r[v : v + 1, :] + low, 0.0
                )
                high = nt_dot(vec, high_b[v])[0:1, 0:1]
                state[v : v + 1, LANES + cells : 2 * LANES + cells] = jnp.where(
                    lane == 0, high_r[v : v + 1, :] + high, 0.0
                )

        for v in range(2):
            both = nt_dot(vec, basis[v])
            state[v : v + 1, inner] = both[0:1] + ref_ref[v : v + 1, here]
            state[v + 2 : v + 3, inner] = both[1:2]

    @pl.when((phase == 1) & (tile == 0))
    def _():
        top[...] = jnp.zeros_like(top)
        bottom[...] = jnp.zeros_like(bottom)
        right[...] = jnp.zeros_like(right)
        full = state[...]
        total = full.shape[1]
        centre = full[:, LANES : LANES + cells]
        left = pltpu.roll(full, 1, 1)[:, LANES : LANES + cells]
        after = pltpu.roll(full, total - 1, 1)[:, LANES : LANES + cells]
        flux = nu * (left - 2.0 * centre + after) - c * (centre - left)
        fuel, heat = centre[0:1], centre[1:2]
        active = burn_ref[...].astype(jnp.float32)
        tangent = jnp.tanh(heat)
        slope_fuel = k * active * (1.0 + tangent)
        slope_heat = k * active * fuel * (1.0 - tangent * tangent)
        reaction = k * active * fuel * (1.0 + tangent)
        res_fuel = centre[2:3] - h * (flux[0:1] - reaction)
        res_heat = centre[3:4] - h * (flux[1:2] + reaction)
        res_out[0:1, :] = res_fuel
        res_out[1:2, :] = res_heat
        resid[0:1, :] = res_fuel
        resid[1:2, :] = res_heat
        row = lax.broadcasted_iota(jnp.int32, (8, cells), 0)
        stacked = jnp.where(row == 0, h * slope_fuel, jnp.where(row == 1, h * slope_heat, 0.0))
        for part in range(cells // LANES):
            span = slice(part * LANES, (part + 1) * LANES)
            coef[span, :] = stacked[:, span].T

    @pl.when(phase == 1)
    def _():
        for v in range(2):
            wide[v, 8 : 8 + TILE, :] = basis[v].astype(jnp.float32)
            before = jnp.where(tile == 0, low_b[v], before_rows[v]).astype(jnp.float32)
            wide[v, 0:8, :] = before[EDGE - 8 : EDGE]
            after = jnp.where(tile == tiles - 1, high_b[v], after_rows[v]).astype(jnp.float32)
            wide[v, 8 + TILE : 16 + TILE, :] = after[0:8]
        base = 1.0 + 2.0 * h * nu + h * c
        to_left = -h * (nu + c)
        to_right = -h * nu

        for start in range(0, TILE, ROWS):
            at = pl.ds(pl.multiple_of(tile * TILE + start, ROWS), ROWS)
            pair = coef[at, :]
            ha, he = pair[:, 0:1], pair[:, 1:2]
            centre, side = [], []
            for v in range(2):
                centre.append(wide[v, 8 + start : 8 + start + ROWS, :])
                side.append(
                    to_left * wide[v, 7 + start : 7 + start + ROWS, :]
                    + to_right * wide[v, 9 + start : 9 + start + ROWS, :]
                )
            fuel_rows = (base + ha) * centre[0] + side[0] + he * centre[1]
            heat_rows = (base - he) * centre[1] + side[1] - ha * centre[0]
            jac[0, start : start + ROWS, :] = fuel_rows.astype(jnp.bfloat16)
            jac[1, start : start + ROWS, :] = heat_rows.astype(jnp.bfloat16)

        rows = jac[...].reshape(2 * TILE, modes)
        top[...] += tn_dot(rows[:, 0:half], rows)
        bottom[...] += tn_dot(rows[:, half:], rows[:, half:])
        both = resid[:, here].astype(jnp.bfloat16)
        part_fuel = jnp.dot(both, jac[0], preferred_element_type=jnp.float32)
        part_heat = jnp.dot(both, jac[1], preferred_element_type=jnp.float32)
        right[...] += part_fuel[0:1] + part_heat[1:2]

    @pl.when((phase == 1) & (tile == tiles - 1))
    def _():
        blocks = modes // LANES
        spot = 0
        for i in range(blocks):
            for j in range(i, blocks):
                if i * LANES < half:
                    block = top[i * LANES : (i + 1) * LANES, j * LANES : (j + 1) * LANES]
                else:
                    a, b = i * LANES - half, j * LANES - half
                    block = bottom[a : a + LANES, b : b + LANES]
                packed[spot * LANES : (spot + 1) * LANES, :] = block
                spot += 1
        used = spot * LANES
        packed[used:, :] = jnp.zeros((packed.shape[0] - used, LANES), jnp.float32)
        for i in range(blocks):
            packed[used + i : used + i + 1, :] = right[:, i * LANES : (i + 1) * LANES]


def assemble(packed_rows, params, coords_now, coords_before, ref, burning, basis, edges):
    cells, modes = basis.shape[1:]
    tiles = cells // TILE
    per = TILE // EDGE
    last = cells // EDGE - 1
    smem = pl.BlockSpec(memory_space=pltpu.SMEM)
    vmem = pl.BlockSpec(memory_space=pltpu.VMEM)
    half = modes // 2
    return pl.pallas_call(
        main_kernel,
        grid=(2, tiles),
        out_shape=[
            jax.ShapeDtypeStruct((2, cells, modes), jnp.bfloat16),
            jax.ShapeDtypeStruct((2, cells), jnp.float32),
            jax.ShapeDtypeStruct((packed_rows, LANES), jnp.float32),
        ],
        in_specs=[smem] * 3
        + [vmem] * 4
        + [
            pl.BlockSpec((2, TILE, modes), lambda p, i: (0, i, 0)),
            pl.BlockSpec((2, EDGE, modes), lambda p, i: (0, jnp.maximum(i * per - 1, 0), 0)),
            pl.BlockSpec((2, EDGE, modes), lambda p, i: (0, jnp.minimum((i + 1) * per, last), 0)),
        ]
        + [vmem] * 4,
        out_specs=[
            pl.BlockSpec((2, TILE, modes), lambda p, i: (0, i * p, 0)),
            vmem,
            vmem,
        ],
        scratch_shapes=[
            pltpu.VMEM((8, cells + 2 * LANES), jnp.float32),
            pltpu.VMEM((cells, 8), jnp.float32),
            pltpu.VMEM((16, cells), jnp.float32),
            pltpu.VMEM((2, TILE + 16, modes), jnp.float32),
            pltpu.VMEM((half, modes), jnp.float32),
            pltpu.VMEM((half, half), jnp.float32),
            pltpu.VMEM((1, modes), jnp.float32),
        ],
        compiler_params=pltpu.CompilerParams(vmem_limit_bytes=48 * 2**20),
    )(*params, coords_now, coords_before, ref, burning, basis, basis, basis, *edges)


def sum_kernel(n, part, out, arrived, gathered, send_a, recv_a, send_b, recv_b):
    me = lax.axis_index("space")
    size = part.shape[0] // n
    barrier = pltpu.get_barrier_semaphore()

    def greet(o, carry):
        pl.semaphore_signal(
            barrier, inc=1, device_id={"space": lax.rem(me + o, n)}, device_id_type=MESH
        )
        return carry

    lax.fori_loop(1, n, greet, 0)
    pl.semaphore_wait(barrier, n - 1)

    def span(d):
        return pl.ds(pl.multiple_of(d * size, 8), size)

    def scatter(o):
        to = lax.rem(me + o, n)
        return pltpu.make_async_remote_copy(
            src_ref=part.at[span(to)],
            dst_ref=arrived.at[o - 1],
            send_sem=send_a.at[o - 1],
            recv_sem=recv_a.at[o - 1],
            device_id={"space": to},
            device_id_type=MESH,
        )

    def gather(o, owner):
        return pltpu.make_async_remote_copy(
            src_ref=gathered.at[span(owner)],
            dst_ref=gathered.at[span(owner)],
            send_sem=send_b.at[o - 1],
            recv_sem=recv_b.at[o - 1],
            device_id={"space": lax.rem(me + o, n)},
            device_id_type=MESH,
        )

    def start_scatter(o, carry):
        scatter(o).start()
        return carry

    def take(o, total):
        scatter(o).wait_recv()
        return total + arrived[o - 1]

    def start_gather(o, carry):
        gather(o, me).start()
        return carry

    def finish(o, carry):
        scatter(o).wait_send()
        gather(o, me).wait_send()
        gather(o, lax.rem(me + n - o, n)).wait_recv()
        return carry

    lax.fori_loop(1, n, start_scatter, 0)
    gathered[span(me), :] = lax.fori_loop(1, n, take, part[span(me), :])
    lax.fori_loop(1, n, start_gather, 0)
    lax.fori_loop(1, n, finish, 0)
    out[...] = gathered[...]


def sum_over_space(n, part):
    rows = part.shape[0]
    dma = pltpu.SemaphoreType.DMA((n - 1,))
    vmem = pl.BlockSpec(memory_space=pltpu.VMEM)
    return pl.pallas_call(
        functools.partial(sum_kernel, n),
        out_shape=jax.ShapeDtypeStruct(part.shape, jnp.float32),
        in_specs=[vmem],
        out_specs=vmem,
        scratch_shapes=[
            pltpu.VMEM((n - 1, rows // n, LANES), jnp.float32),
            pltpu.VMEM(part.shape, jnp.float32),
            dma,
            dma,
            dma,
            dma,
        ],
        compiler_params=pltpu.CompilerParams(
            collective_id=1, has_side_effects=True, vmem_limit_bytes=32 * 2**20
        ),
    )(part)


PANEL = 8


def factor_panel(work, p, scaled, plain):
    first = p * PANEL
    rows = work[first : first + PANEL, :]
    a = [rows[i : i + 1, 0:LANES] for i in range(PANEL)]
    w = [rows[i : i + 1, LANES:] for i in range(PANEL)]
    s = {
        (i, j): jnp.broadcast_to(a[i][:, first + j : first + j + 1], (1, LANES))
        for i in range(PANEL)
        for j in range(i, PANEL)
    }
    for k in range(PANEL):
        inverse = 1.0 / s[k, k]
        for i in range(k + 1, PANEL):
            m = s[k, i] * inverse
            for j in range(i, PANEL):
                s[i, j] = s[i, j] - m * s[k, j]
            a[i] = a[i] - m * a[k]
            w[i] = w[i] - m * w[k]
        plain[first + k : first + k + 1, 0:LANES] = a[k]
        plain[first + k : first + k + 1, LANES:] = w[k]
        scaled[first + k : first + k + 1, 0:LANES] = a[k] * inverse
        scaled[first + k : first + k + 1, LANES:] = w[k] * inverse
    below = first + PANEL
    if below < LANES:
        change = tn_dot(
            scaled[first:below, 0:LANES], plain[first:below, :], HIGH
        )
        work[below:, :] = work[below:, :] - change[below:, :]


def solve_kernel(modes, packed, out, blocks, work, scaled, plain):
    count = modes // LANES
    place = {}
    for i in range(count):
        for j in range(i, count):
            place[i, j] = len(place)
            blocks[place[i, j]] = packed[place[i, j] * LANES : (place[i, j] + 1) * LANES, :]
    used = len(place) * LANES
    b = [packed[used + i : used + i + 1, :] for i in range(count)]
    row = lax.broadcasted_iota(jnp.int32, (LANES, LANES), 0)
    col = lax.broadcasted_iota(jnp.int32, (LANES, LANES), 1)
    eye = jnp.where(row == col, 1.0, 0.0).astype(jnp.float32)
    z, forward = [], {}
    for k in range(count):
        work[:, 0:LANES] = blocks[place[k, k]]
        work[:, LANES:] = eye
        for p in range(LANES // PANEL):
            factor_panel(work, p, scaled, plain)
        inverse = tn_dot(scaled[:, LANES:], plain[:, LANES:], HIGH)
        z.append(jnp.dot(b[k], inverse, precision=HIGH, preferred_element_type=jnp.float32))
        for j in range(k + 1, count):
            forward[k, j] = jnp.dot(
                inverse, blocks[place[k, j]], precision=HIGH, preferred_element_type=jnp.float32
            )
        for j in range(k + 1, count):
            b[j] = b[j] - jnp.dot(
                z[k], blocks[place[k, j]], precision=HIGH, preferred_element_type=jnp.float32
            )
            for i in range(k + 1, j + 1):
                blocks[place[i, j]] = blocks[place[i, j]] - tn_dot(
                    blocks[place[k, i]], forward[k, j], HIGH
                )
    x = [None] * count
    for k in reversed(range(count)):
        x[k] = z[k]
        for j in range(k + 1, count):
            x[k] = x[k] - nt_dot(x[j], forward[k, j], HIGH)
        out[:, k * LANES : (k + 1) * LANES] = -x[k]


def solve(modes, packed):
    count = modes // LANES
    vmem = pl.BlockSpec(memory_space=pltpu.VMEM)
    return pl.pallas_call(
        functools.partial(solve_kernel, modes),
        out_shape=jax.ShapeDtypeStruct((1, modes), jnp.float32),
        in_specs=[vmem],
        out_specs=vmem,
        scratch_shapes=[
            pltpu.VMEM((count * (count + 1) // 2, LANES, LANES), jnp.float32),
            pltpu.VMEM((LANES, 2 * LANES), jnp.float32),
            pltpu.VMEM((LANES, 2 * LANES), jnp.float32),
            pltpu.VMEM((LANES, 2 * LANES), jnp.float32),
        ],
        compiler_params=pltpu.CompilerParams(vmem_limit_bytes=32 * 2**20),
    )(packed)


def on_device(
    basis_rows,
    reference_state,
    burning,
    coords_now,
    coords_before,
    diffusivity,
    advection,
    reaction_rate,
):
    n = lax.axis_size("space")
    modes = basis_rows.shape[2]
    blocks = modes // LANES
    needed = blocks * (blocks + 1) // 2 * LANES + 8
    share = -(-needed // (8 * n)) * 8
    edges = halo(n, basis_rows, reference_state)
    jacobian, residual, packed = assemble(
        share * n,
        (diffusivity, advection, reaction_rate),
        coords_now,
        coords_before,
        reference_state,
        burning[None],
        basis_rows,
        edges,
    )
    update = solve(modes, sum_over_space(n, packed))
    return (jacobian[None], residual[None], update)


def solution(mesh):
    in_specs = (
        P(None, "space", None),
        P(None, "space"),
        P("space"),
        P("inst", None),
        P("inst", None),
        P("inst"),
        P("inst"),
        P("inst"),
    )
    out_specs = (P("inst", None, "space", None), P("inst", None, "space"), P("inst", None))
    return jax.shard_map(
        on_device, mesh=mesh, in_specs=in_specs, out_specs=out_specs, check_vma=False
    )
```

```python
import functools

import jax
import jax.numpy as jnp
from jax import lax
from jax.experimental import pallas as pl
from jax.experimental.pallas import tpu as pltpu
from jax.sharding import PartitionSpec as P

time_step = 0.5
MESH = pl.DeviceIdType.MESH
TILE = 512
ROWS = 32
LANES = 128
EDGE = 16
HIGH = lax.Precision.HIGHEST
PANEL = 8
RIGHT_STAGE = 1


def tn_dot(a, b, precision=None):
    return lax.dot_general(
        a, b, (((0,), (0,)), ((), ())), preferred_element_type=jnp.float32, precision=precision
    )


def nt_dot(a, b, precision=None):
    return lax.dot_general(
        a, b, (((1,), (1,)), ((), ())), preferred_element_type=jnp.float32, precision=precision
    )


def halo_kernel(n, basis, ref, low_b, high_b, low_r, high_r, send, recv):
    me = lax.axis_index("space")
    cells = basis.shape[1]
    has_low, has_high = me > 0, me < n - 1

    low_b[...] = jnp.zeros_like(low_b)
    high_b[...] = jnp.zeros_like(high_b)
    low_r[...] = jnp.zeros_like(low_r)
    high_r[...] = jnp.zeros_like(high_r)

    barrier = pltpu.get_barrier_semaphore()
    for step in (1, n - 1):
        pl.semaphore_signal(
            barrier, inc=1, device_id={"space": lax.rem(me + step, n)}, device_id_type=MESH
        )
    pl.semaphore_wait(barrier, 2)

    up = {"space": lax.rem(me + 1, n)}
    down = {"space": lax.rem(me + n - 1, n)}

    def copy(src, dst, slot, target):
        return pltpu.make_async_remote_copy(
            src_ref=src,
            dst_ref=dst,
            send_sem=send.at[slot],
            recv_sem=recv.at[slot],
            device_id=target,
            device_id_type=MESH,
        )

    to_up = [
        copy(basis.at[:, pl.ds(cells - EDGE, EDGE), :], low_b, 0, up),
        copy(ref.at[:, pl.ds(cells - LANES, LANES)], low_r, 1, up),
    ]
    to_down = [
        copy(basis.at[:, pl.ds(0, EDGE), :], high_b, 2, down),
        copy(ref.at[:, pl.ds(0, LANES)], high_r, 3, down),
    ]

    @pl.when(has_high)
    def _():
        for c in to_up:
            c.start()

    @pl.when(has_low)
    def _():
        for c in to_down:
            c.start()

    @pl.when(has_high)
    def _():
        for c in to_up:
            c.wait_send()
        for c in to_down:
            c.wait_recv()

    @pl.when(has_low)
    def _():
        for c in to_down:
            c.wait_send()
        for c in to_up:
            c.wait_recv()


def halo(n, basis, ref):
    modes = basis.shape[2]
    vmem = pl.BlockSpec(memory_space=pltpu.VMEM)
    return pl.pallas_call(
        functools.partial(halo_kernel, n),
        out_shape=[
            jax.ShapeDtypeStruct((2, EDGE, modes), jnp.bfloat16),
            jax.ShapeDtypeStruct((2, EDGE, modes), jnp.bfloat16),
            jax.ShapeDtypeStruct((2, LANES), jnp.float32),
            jax.ShapeDtypeStruct((2, LANES), jnp.float32),
        ],
        in_specs=[pl.BlockSpec(memory_space=pl.ANY)] * 2,
        out_specs=[vmem] * 4,
        scratch_shapes=[pltpu.SemaphoreType.DMA((4,)), pltpu.SemaphoreType.DMA((4,))],
        compiler_params=pltpu.CompilerParams(collective_id=0, has_side_effects=True),
    )(basis, ref)


def main_kernel(
    stages, diffusivity, advection, rate, now_ref, before_ref, ref_ref, burn_ref, basis, before_rows,
    after_rows, low_b, high_b, low_r, high_r,
    jac, res_out, packed,
    state, coef, resid, wide, top, bottom, right,
):
    phase, tile = pl.program_id(0), pl.program_id(1)
    tiles = pl.num_programs(1)
    cells = res_out.shape[1]
    modes = basis.shape[2]
    half = modes // 2
    here = pl.ds(pl.multiple_of(tile * TILE, TILE), TILE)
    inner = pl.ds(pl.multiple_of(tile * TILE + LANES, LANES), TILE)
    h = time_step
    nu, c, k = diffusivity[0], advection[0], rate[0]

    def coords():
        now, old = now_ref[...], before_ref[...]
        row = lax.broadcasted_iota(jnp.int32, (16, modes), 0)
        both = jnp.where(row == 0, now, jnp.where(row == 1, now - old, 0.0))
        return both.astype(jnp.bfloat16)

    @pl.when(phase == 0)
    def _():
        vec = coords()

        @pl.when(tile == 0)
        def _():
            state[...] = jnp.zeros_like(state)
            resid[...] = jnp.zeros_like(resid)
            lane = lax.broadcasted_iota(jnp.int32, (1, LANES), 1)
            for v in range(2):
                low = nt_dot(vec, low_b[v])[0:1, EDGE - 1 : EDGE]
                state[v : v + 1, 0:LANES] = jnp.where(
                    lane == LANES - 1, low_r[v : v + 1, :] + low, 0.0
                )
                high = nt_dot(vec, high_b[v])[0:1, 0:1]
                state[v : v + 1, LANES + cells : 2 * LANES + cells] = jnp.where(
                    lane == 0, high_r[v : v + 1, :] + high, 0.0
                )

        for v in range(2):
            both = nt_dot(vec, basis[v])
            state[v : v + 1, inner] = both[0:1] + ref_ref[v : v + 1, here]
            state[v + 2 : v + 3, inner] = both[1:2]

    @pl.when((phase == 1) & (tile == 0))
    def _():
        top[...] = jnp.zeros_like(top)
        bottom[...] = jnp.zeros_like(bottom)
        right[...] = jnp.zeros_like(right)
        full = state[...]
        total = full.shape[1]
        centre = full[:, LANES : LANES + cells]
        left = pltpu.roll(full, 1, 1)[:, LANES : LANES + cells]
        after = pltpu.roll(full, total - 1, 1)[:, LANES : LANES + cells]
        flux = nu * (left - 2.0 * centre + after) - c * (centre - left)
        fuel, heat = centre[0:1], centre[1:2]
        active = burn_ref[...].astype(jnp.float32)
        tangent = jnp.tanh(heat)
        slope_fuel = k * active * (1.0 + tangent)
        slope_heat = k * active * fuel * (1.0 - tangent * tangent)
        reaction = k * active * fuel * (1.0 + tangent)
        res_fuel = centre[2:3] - h * (flux[0:1] - reaction)
        res_heat = centre[3:4] - h * (flux[1:2] + reaction)
        res_out[0:1, :] = res_fuel
        res_out[1:2, :] = res_heat
        resid[0:1, :] = res_fuel
        resid[1:2, :] = res_heat
        row = lax.broadcasted_iota(jnp.int32, (8, cells), 0)
        stacked = jnp.where(row == 0, h * slope_fuel, jnp.where(row == 1, h * slope_heat, 0.0))
        for part in range(cells // LANES):
            span = slice(part * LANES, (part + 1) * LANES)
            coef[span, :] = stacked[:, span].T

    @pl.when(phase == 1)
    def _():
        for v in range(2):
            wide[v, 8 : 8 + TILE, :] = basis[v].astype(jnp.float32)
            before = jnp.where(tile == 0, low_b[v], before_rows[v]).astype(jnp.float32)
            wide[v, 0:8, :] = before[EDGE - 8 : EDGE]
            after = jnp.where(tile == tiles - 1, high_b[v], after_rows[v]).astype(jnp.float32)
            wide[v, 8 + TILE : 16 + TILE, :] = after[0:8]
        base = 1.0 + 2.0 * h * nu + h * c
        to_left = -h * (nu + c)
        to_right = -h * nu

        for start in range(0, TILE, ROWS):
            at = pl.ds(pl.multiple_of(tile * TILE + start, ROWS), ROWS)
            pair = coef[at, :]
            ha, he = pair[:, 0:1], pair[:, 1:2]
            centre, side = [], []
            for v in range(2):
                centre.append(wide[v, 8 + start : 8 + start + ROWS, :])
                side.append(
                    to_left * wide[v, 7 + start : 7 + start + ROWS, :]
                    + to_right * wide[v, 9 + start : 9 + start + ROWS, :]
                )
            fuel_rows = (base + ha) * centre[0] + side[0] + he * centre[1]
            heat_rows = (base - he) * centre[1] + side[1] - ha * centre[0]
            jac[0, start : start + ROWS, :] = fuel_rows.astype(jnp.bfloat16)
            jac[1, start : start + ROWS, :] = heat_rows.astype(jnp.bfloat16)

        rows = jac[...].reshape(2 * TILE, modes)
        top[...] += tn_dot(rows[:, 0:half], rows)
        bottom[...] += tn_dot(rows[:, half:], rows[:, half:])
        both = resid[:, here].astype(jnp.bfloat16)
        part_fuel = jnp.dot(both, jac[0], preferred_element_type=jnp.float32)
        part_heat = jnp.dot(both, jac[1], preferred_element_type=jnp.float32)
        right[...] += part_fuel[0:1] + part_heat[1:2]

    @pl.when((phase == 1) & (tile == tiles - 1))
    def _():
        packed[...] = jnp.zeros_like(packed)
        for stage, (offset, _) in enumerate(stages):
            j = stage
            for i in range(j + 1):
                if i * LANES < half:
                    block = top[i * LANES : (i + 1) * LANES, j * LANES : (j + 1) * LANES]
                else:
                    first, second = i * LANES - half, j * LANES - half
                    block = bottom[first : first + LANES, second : second + LANES]
                packed[offset + i * LANES : offset + (i + 1) * LANES, :] = block
        used = stages[RIGHT_STAGE][0] + (RIGHT_STAGE + 1) * LANES
        for i in range(modes // LANES):
            packed[used + i : used + i + 1, :] = right[:, i * LANES : (i + 1) * LANES]


def assemble(stages, packed_rows, params, coords_now, coords_before, ref, burning, basis, edges):
    cells, modes = basis.shape[1:]
    tiles = cells // TILE
    per = TILE // EDGE
    last = cells // EDGE - 1
    smem = pl.BlockSpec(memory_space=pltpu.SMEM)
    vmem = pl.BlockSpec(memory_space=pltpu.VMEM)
    half = modes // 2

    def whole(array):
        return pl.BlockSpec(array.shape, lambda p, i: (0,) * array.ndim)

    return pl.pallas_call(
        functools.partial(main_kernel, stages),
        grid=(2, tiles),
        out_shape=[
            jax.ShapeDtypeStruct((2, cells, modes), jnp.bfloat16),
            jax.ShapeDtypeStruct((2, cells), jnp.float32),
            jax.ShapeDtypeStruct((packed_rows, LANES), jnp.float32),
        ],
        in_specs=[smem] * 3
        + [whole(coords_now), whole(coords_before), whole(ref), whole(burning)]
        + [
            pl.BlockSpec((2, TILE, modes), lambda p, i: (0, i, 0)),
            pl.BlockSpec((2, EDGE, modes), lambda p, i: (0, jnp.maximum(i * per - 1, 0), 0)),
            pl.BlockSpec((2, EDGE, modes), lambda p, i: (0, jnp.minimum((i + 1) * per, last), 0)),
        ]
        + [whole(edge) for edge in edges],
        out_specs=[
            pl.BlockSpec((2, TILE, modes), lambda p, i: (0, i * p, 0)),
            vmem,
            vmem,
        ],
        scratch_shapes=[
            pltpu.VMEM((8, cells + 2 * LANES), jnp.float32),
            pltpu.VMEM((cells, 8), jnp.float32),
            pltpu.VMEM((16, cells), jnp.float32),
            pltpu.VMEM((2, TILE + 16, modes), jnp.float32),
            pltpu.VMEM((half, modes), jnp.float32),
            pltpu.VMEM((half, half), jnp.float32),
            pltpu.VMEM((1, modes), jnp.float32),
        ],
        compiler_params=pltpu.CompilerParams(vmem_limit_bytes=48 * 2**20),
    )(*params, coords_now, coords_before, ref, burning, basis, basis, basis, *edges)


def layout(n, modes):
    stages, offset = [], 0
    for j in range(modes // LANES):
        needed = (j + 1) * LANES + (8 if j == RIGHT_STAGE else 0)
        size = -(-needed // (8 * n)) * 8
        stages.append((offset, size))
        offset += size * n
    return tuple(stages), offset


def sum_solve_kernel(
    n, stages, modes, part, out,
    arrived, total, work, panel_a, panel_w, plain, scaled, send_a, recv_a, send_b, recv_b,
):
    me = lax.axis_index("space")
    barrier = pltpu.get_barrier_semaphore()

    def greet(o, carry):
        pl.semaphore_signal(
            barrier, inc=1, device_id={"space": lax.rem(me + o, n)}, device_id_type=MESH
        )
        return carry

    lax.fori_loop(1, n, greet, 0)
    pl.semaphore_wait(barrier, n - 1)

    def span(stage, d):
        offset, size = stages[stage]
        return pl.ds(pl.multiple_of(offset + d * size, 8), size)

    def scatter(stage, o):
        to = lax.rem(me + o, n)
        offset, size = stages[stage]
        return pltpu.make_async_remote_copy(
            src_ref=part.at[span(stage, to)],
            dst_ref=arrived.at[o - 1, pl.ds(offset // n, size)],
            send_sem=send_a.at[stage, o - 1],
            recv_sem=recv_a.at[stage, o - 1],
            device_id={"space": to},
            device_id_type=MESH,
        )

    def gather(stage, o, owner):
        return pltpu.make_async_remote_copy(
            src_ref=total.at[span(stage, owner)],
            dst_ref=total.at[span(stage, owner)],
            send_sem=send_b.at[stage, o - 1],
            recv_sem=recv_b.at[stage, o - 1],
            device_id={"space": lax.rem(me + o, n)},
            device_id_type=MESH,
        )

    def start_sum(stage):
        def body(o, carry):
            scatter(stage, o).start()
            return carry

        lax.fori_loop(1, n, body, 0)

    def pass_on(stage):
        offset, size = stages[stage]

        def add(o, sums):
            scatter(stage, o).wait_recv()
            return sums + arrived[o - 1, offset // n : offset // n + size, :]

        def send(o, carry):
            gather(stage, o, me).start()
            return carry

        total[span(stage, me), :] = lax.fori_loop(1, n, add, part[span(stage, me), :])
        lax.fori_loop(1, n, send, 0)

    def end_sum(stage):
        def body(o, carry):
            scatter(stage, o).wait_send()
            gather(stage, o, me).wait_send()
            gather(stage, o, lax.rem(me + n - o, n)).wait_recv()
            return carry

        lax.fori_loop(1, n, body, 0)

    lane = lax.broadcasted_iota(jnp.int32, (PANEL, LANES), 1)

    def factor_panel(p, carry):
        first = pl.multiple_of(p * PANEL, PANEL)
        rows_a = work[pl.ds(first, PANEL), 0:LANES]
        rows_w = work[pl.ds(first, PANEL), LANES:]
        turned = pltpu.roll(rows_a, LANES - first, 1)
        a = [rows_a[i : i + 1, :] for i in range(PANEL)]
        w = [rows_w[i : i + 1, :] for i in range(PANEL)]
        s = {
            (i, j): jnp.broadcast_to(turned[i : i + 1, j : j + 1], (1, LANES))
            for i in range(PANEL)
            for j in range(i, PANEL)
        }
        for k in range(PANEL):
            inverse = 1.0 / s[k, k]
            for i in range(k + 1, PANEL):
                m = s[k, i] * inverse
                for j in range(i, PANEL):
                    s[i, j] = s[i, j] - m * s[k, j]
                a[i] = a[i] - m * a[k]
                w[i] = w[i] - m * w[k]
            panel_a[k : k + 1, :] = a[k] * inverse
            panel_w[k : k + 1, 0:LANES] = a[k]
            panel_w[k : k + 1, LANES:] = w[k]
            panel_w[PANEL + k : PANEL + k + 1, LANES:] = w[k] * inverse
        both = panel_w[0:PANEL, :]
        plain[pl.ds(first, PANEL), :] = both[:, LANES:]
        scaled[pl.ds(first, PANEL), :] = panel_w[PANEL:, LANES:]
        below = jnp.where(lane >= first + PANEL, panel_a[...], 0.0)
        work[...] = work[...] - tn_dot(below, both, HIGH)
        return carry

    def factor(low, high):
        lax.fori_loop(low, high, factor_panel, 0)

    def block(i, j):
        return total[stages[j][0] + i * LANES : stages[j][0] + (i + 1) * LANES, :]

    def dot(a, b):
        return jnp.dot(a, b, precision=HIGH, preferred_element_type=jnp.float32)

    count = modes // LANES
    panels = LANES // PANEL
    row = lax.broadcasted_iota(jnp.int32, (LANES, LANES), 0)
    col = lax.broadcasted_iota(jnp.int32, (LANES, LANES), 1)
    eye = jnp.where(row == col, 1.0, 0.0).astype(jnp.float32)

    between = {(0, 4): [1], (0, 10): [2], (1, 6): [3]}
    start_sum(0)
    start_sum(1)
    pass_on(0)
    start_sum(2)
    start_sum(3)

    inverses, upper, forward, z, b = [], {}, {}, [], None
    for k in range(count):
        end_sum(k)
        if k == RIGHT_STAGE:
            used = stages[k][0] + (k + 1) * LANES
            b = [total[used + i : used + i + 1, :] for i in range(count)]
        for i in range(k + 1):
            current = block(i, k)
            for r in range(i):
                current = current - tn_dot(upper[r, i], forward[r, k], HIGH)
            if i < k:
                upper[i, k] = current
                forward[i, k] = dot(inverses[i], current)
        work[:, 0:LANES] = current
        work[:, LANES:] = eye
        done = 0
        for at in range(1, panels):
            for stage in between.get((k, at), ()):
                factor(done, at)
                pass_on(stage)
                done = at
        factor(done, panels)
        inverses.append(tn_dot(scaled[...], plain[...], HIGH))
    for k in range(count):
        current = b[k]
        for r in range(k):
            current = current - dot(z[r], upper[r, k])
        z.append(dot(current, inverses[k]))
    x = [None] * count
    for k in reversed(range(count)):
        x[k] = z[k]
        for j in range(k + 1, count):
            x[k] = x[k] - nt_dot(x[j], forward[k, j], HIGH)
        out[:, k * LANES : (k + 1) * LANES] = -x[k]


def sum_and_solve(n, stages, modes, part):
    rows = part.shape[0]
    dma = pltpu.SemaphoreType.DMA((len(stages), n - 1))
    vmem = pl.BlockSpec(memory_space=pltpu.VMEM)
    return pl.pallas_call(
        functools.partial(sum_solve_kernel, n, stages, modes),
        out_shape=jax.ShapeDtypeStruct((1, modes), jnp.float32),
        in_specs=[vmem],
        out_specs=vmem,
        scratch_shapes=[
            pltpu.VMEM((n - 1, rows // n, LANES), jnp.float32),
            pltpu.VMEM((rows, LANES), jnp.float32),
            pltpu.VMEM((LANES, 2 * LANES), jnp.float32),
            pltpu.VMEM((PANEL, LANES), jnp.float32),
            pltpu.VMEM((2 * PANEL, 2 * LANES), jnp.float32),
            pltpu.VMEM((LANES, LANES), jnp.float32),
            pltpu.VMEM((LANES, LANES), jnp.float32),
            dma,
            dma,
            dma,
            dma,
        ],
        compiler_params=pltpu.CompilerParams(
            collective_id=1, has_side_effects=True, vmem_limit_bytes=32 * 2**20
        ),
    )(part)


def on_device(
    basis_rows,
    reference_state,
    burning,
    coords_now,
    coords_before,
    diffusivity,
    advection,
    reaction_rate,
):
    n = lax.axis_size("space")
    modes = basis_rows.shape[2]
    stages, packed_rows = layout(n, modes)
    edges = halo(n, basis_rows, reference_state)
    jacobian, residual, packed = assemble(
        stages,
        packed_rows,
        (diffusivity, advection, reaction_rate),
        coords_now,
        coords_before,
        reference_state,
        burning[None],
        basis_rows,
        edges,
    )
    update = sum_and_solve(n, stages, modes, packed)
    return (jacobian[None], residual[None], update)


def solution(mesh):
    in_specs = (
        P(None, "space", None),
        P(None, "space"),
        P("space"),
        P("inst", None),
        P("inst", None),
        P("inst"),
        P("inst"),
        P("inst"),
    )
    out_specs = (P("inst", None, "space", None), P("inst", None, "space"), P("inst", None))
    return jax.shard_map(
        on_device, mesh=mesh, in_specs=in_specs, out_specs=out_specs, check_vma=False
    )
```

```python
import functools

import jax
import jax.numpy as jnp
from jax import lax
from jax.experimental import pallas as pl
from jax.experimental.pallas import tpu as pltpu
from jax.sharding import PartitionSpec as P

time_step = 0.5
MESH = pl.DeviceIdType.MESH
TILE = 512
ROWS = 32
LANES = 128
EDGE = 16
HIGH = lax.Precision.HIGHEST
PANEL = 16
RIGHT_STAGE = 1


def tn_dot(a, b, precision=None):
    return lax.dot_general(
        a, b, (((0,), (0,)), ((), ())), preferred_element_type=jnp.float32, precision=precision
    )


def nt_dot(a, b, precision=None):
    return lax.dot_general(
        a, b, (((1,), (1,)), ((), ())), preferred_element_type=jnp.float32, precision=precision
    )


def reciprocal(x):
    guess = pl.reciprocal(x, approx=True)
    guess = guess + guess * (1.0 - x * guess)
    return guess + guess * (1.0 - x * guess)


def halo_kernel(n, basis, ref, edge_b, edge_r, send, recv):
    me = lax.axis_index("space")
    cells = basis.shape[1]
    has_low, has_high = me > 0, me < n - 1

    edge_b[...] = jnp.zeros_like(edge_b)
    edge_r[...] = jnp.zeros_like(edge_r)

    barrier = pltpu.get_barrier_semaphore()
    for step in (1, n - 1):
        pl.semaphore_signal(
            barrier, inc=1, device_id={"space": lax.rem(me + step, n)}, device_id_type=MESH
        )
    pl.semaphore_wait(barrier, 2)

    up = {"space": lax.rem(me + 1, n)}
    down = {"space": lax.rem(me + n - 1, n)}

    def copy(src, dst, slot, target):
        return pltpu.make_async_remote_copy(
            src_ref=src,
            dst_ref=dst,
            send_sem=send.at[slot],
            recv_sem=recv.at[slot],
            device_id=target,
            device_id_type=MESH,
        )

    to_up = [
        copy(basis.at[:, pl.ds(cells - EDGE, EDGE), :], edge_b.at[0], 0, up),
        copy(ref.at[:, pl.ds(cells - LANES, LANES)], edge_r.at[0], 1, up),
    ]
    to_down = [
        copy(basis.at[:, pl.ds(0, EDGE), :], edge_b.at[1], 2, down),
        copy(ref.at[:, pl.ds(0, LANES)], edge_r.at[1], 3, down),
    ]

    @pl.when(has_high)
    def _():
        for c in to_up:
            c.start()

    @pl.when(has_low)
    def _():
        for c in to_down:
            c.start()

    @pl.when(has_high)
    def _():
        for c in to_up:
            c.wait_send()
        for c in to_down:
            c.wait_recv()

    @pl.when(has_low)
    def _():
        for c in to_down:
            c.wait_send()
        for c in to_up:
            c.wait_recv()


def halo(n, basis, ref):
    modes = basis.shape[2]
    vmem = pl.BlockSpec(memory_space=pltpu.VMEM)
    return pl.pallas_call(
        functools.partial(halo_kernel, n),
        out_shape=[
            jax.ShapeDtypeStruct((2, 2, EDGE, modes), jnp.bfloat16),
            jax.ShapeDtypeStruct((2, 2, LANES), jnp.float32),
        ],
        in_specs=[pl.BlockSpec(memory_space=pl.ANY)] * 2,
        out_specs=[vmem] * 2,
        scratch_shapes=[pltpu.SemaphoreType.DMA((4,)), pltpu.SemaphoreType.DMA((4,))],
        compiler_params=pltpu.CompilerParams(collective_id=0, has_side_effects=True),
    )(basis, ref)


def main_kernel(
    stages, diffusivity, advection, rate, now_ref, before_ref, ref_ref, burn_ref, basis, before_rows,
    after_rows, edge_b, edge_r,
    jac, res_out, packed,
    state, coef, resid, wide, top, bottom, right,
):
    phase, tile = pl.program_id(0), pl.program_id(1)
    tiles = pl.num_programs(1)
    cells = res_out.shape[1]
    modes = basis.shape[2]
    half = modes // 2
    here = pl.ds(pl.multiple_of(tile * TILE, TILE), TILE)
    inner = pl.ds(pl.multiple_of(tile * TILE + LANES, LANES), TILE)
    h = time_step
    nu, c, k = diffusivity[0], advection[0], rate[0]

    def coords():
        now, old = now_ref[...], before_ref[...]
        row = lax.broadcasted_iota(jnp.int32, (16, modes), 0)
        both = jnp.where(row == 0, now, jnp.where(row == 1, now - old, 0.0))
        return both.astype(jnp.bfloat16)

    @pl.when(phase == 0)
    def _():
        vec = coords()

        @pl.when(tile == 0)
        def _():
            state[...] = jnp.zeros_like(state)
            resid[...] = jnp.zeros_like(resid)
            lane = lax.broadcasted_iota(jnp.int32, (1, LANES), 1)
            for v in range(2):
                low = nt_dot(vec, edge_b[0, v])[0:1, EDGE - 1 : EDGE]
                state[v : v + 1, 0:LANES] = jnp.where(
                    lane == LANES - 1, edge_r[0, v : v + 1, :] + low, 0.0
                )
                high = nt_dot(vec, edge_b[1, v])[0:1, 0:1]
                state[v : v + 1, LANES + cells : 2 * LANES + cells] = jnp.where(
                    lane == 0, edge_r[1, v : v + 1, :] + high, 0.0
                )

        for v in range(2):
            both = nt_dot(vec, basis[v])
            state[v : v + 1, inner] = both[0:1] + ref_ref[v : v + 1, here]
            state[v + 2 : v + 3, inner] = both[1:2]

    @pl.when((phase == 1) & (tile == 0))
    def _():
        top[...] = jnp.zeros_like(top)
        bottom[...] = jnp.zeros_like(bottom)
        right[...] = jnp.zeros_like(right)
        full = state[...]
        total = full.shape[1]
        centre = full[:, LANES : LANES + cells]
        left = pltpu.roll(full, 1, 1)[:, LANES : LANES + cells]
        after = pltpu.roll(full, total - 1, 1)[:, LANES : LANES + cells]
        flux = nu * (left - 2.0 * centre + after) - c * (centre - left)
        fuel, heat = centre[0:1], centre[1:2]
        active = burn_ref[...].astype(jnp.float32)
        tangent = jnp.tanh(heat)
        slope_fuel = k * active * (1.0 + tangent)
        slope_heat = k * active * fuel * (1.0 - tangent * tangent)
        reaction = k * active * fuel * (1.0 + tangent)
        res_fuel = centre[2:3] - h * (flux[0:1] - reaction)
        res_heat = centre[3:4] - h * (flux[1:2] + reaction)
        res_out[0:1, :] = res_fuel
        res_out[1:2, :] = res_heat
        resid[0:1, :] = res_fuel
        resid[1:2, :] = res_heat
        row = lax.broadcasted_iota(jnp.int32, (8, cells), 0)
        stacked = jnp.where(row == 0, h * slope_fuel, jnp.where(row == 1, h * slope_heat, 0.0))
        for part in range(cells // LANES):
            span = slice(part * LANES, (part + 1) * LANES)
            coef[span, :] = stacked[:, span].T

    @pl.when(phase == 1)
    def _():
        for v in range(2):
            wide[v, 8 : 8 + TILE, :] = basis[v].astype(jnp.float32)
            before = jnp.where(tile == 0, edge_b[0, v], before_rows[v]).astype(jnp.float32)
            wide[v, 0:8, :] = before[EDGE - 8 : EDGE]
            after = jnp.where(tile == tiles - 1, edge_b[1, v], after_rows[v]).astype(jnp.float32)
            wide[v, 8 + TILE : 16 + TILE, :] = after[0:8]
        base = 1.0 + 2.0 * h * nu + h * c
        to_left = -h * (nu + c)
        to_right = -h * nu

        for start in range(0, TILE, ROWS):
            at = pl.ds(pl.multiple_of(tile * TILE + start, ROWS), ROWS)
            pair = coef[at, :]
            ha, he = pair[:, 0:1], pair[:, 1:2]
            centre, side = [], []
            for v in range(2):
                centre.append(wide[v, 8 + start : 8 + start + ROWS, :])
                side.append(
                    to_left * wide[v, 7 + start : 7 + start + ROWS, :]
                    + to_right * wide[v, 9 + start : 9 + start + ROWS, :]
                )
            fuel_rows = (base + ha) * centre[0] + side[0] + he * centre[1]
            heat_rows = (base - he) * centre[1] + side[1] - ha * centre[0]
            jac[0, start : start + ROWS, :] = fuel_rows.astype(jnp.bfloat16)
            jac[1, start : start + ROWS, :] = heat_rows.astype(jnp.bfloat16)

        rows = jac[...].reshape(2 * TILE, modes)
        top[...] += tn_dot(rows[:, 0:half], rows)
        bottom[...] += tn_dot(rows[:, half:], rows[:, half:])
        both = resid[:, here].astype(jnp.bfloat16)
        part_fuel = jnp.dot(both, jac[0], preferred_element_type=jnp.float32)
        part_heat = jnp.dot(both, jac[1], preferred_element_type=jnp.float32)
        right[...] += part_fuel[0:1] + part_heat[1:2]

    @pl.when((phase == 1) & (tile == tiles - 1))
    def _():
        packed[...] = jnp.zeros_like(packed)
        for stage, (offset, _) in enumerate(stages):
            j = stage
            for i in range(j + 1):
                if i * LANES < half:
                    block = top[i * LANES : (i + 1) * LANES, j * LANES : (j + 1) * LANES]
                else:
                    first, second = i * LANES - half, j * LANES - half
                    block = bottom[first : first + LANES, second : second + LANES]
                packed[offset + i * LANES : offset + (i + 1) * LANES, :] = block
        used = stages[RIGHT_STAGE][0] + (RIGHT_STAGE + 1) * LANES
        for i in range(modes // LANES):
            packed[used + i : used + i + 1, :] = right[:, i * LANES : (i + 1) * LANES]


def assemble(stages, packed_rows, params, coords_now, coords_before, ref, burning, basis, edges):
    cells, modes = basis.shape[1:]
    tiles = cells // TILE
    per = TILE // EDGE
    last = cells // EDGE - 1
    smem = pl.BlockSpec(memory_space=pltpu.SMEM)
    vmem = pl.BlockSpec(memory_space=pltpu.VMEM)
    half = modes // 2

    def whole(array):
        return pl.BlockSpec(array.shape, lambda p, i: (0,) * array.ndim)

    return pl.pallas_call(
        functools.partial(main_kernel, stages),
        grid=(2, tiles),
        out_shape=[
            jax.ShapeDtypeStruct((2, cells, modes), jnp.bfloat16),
            jax.ShapeDtypeStruct((2, cells), jnp.float32),
            jax.ShapeDtypeStruct((packed_rows, LANES), jnp.float32),
        ],
        in_specs=[smem] * 3
        + [whole(coords_now), whole(coords_before), whole(ref), whole(burning)]
        + [
            pl.BlockSpec((2, TILE, modes), lambda p, i: (0, i, 0)),
            pl.BlockSpec((2, EDGE, modes), lambda p, i: (0, jnp.maximum(i * per - 1, 0), 0)),
            pl.BlockSpec((2, EDGE, modes), lambda p, i: (0, jnp.minimum((i + 1) * per, last), 0)),
        ]
        + [whole(edge) for edge in edges],
        out_specs=[
            pl.BlockSpec((2, TILE, modes), lambda p, i: (0, i * p, 0)),
            vmem,
            vmem,
        ],
        scratch_shapes=[
            pltpu.VMEM((8, cells + 2 * LANES), jnp.float32),
            pltpu.VMEM((cells, 8), jnp.float32),
            pltpu.VMEM((16, cells), jnp.float32),
            pltpu.VMEM((2, TILE + 16, modes), jnp.float32),
            pltpu.VMEM((half, modes), jnp.float32),
            pltpu.VMEM((half, half), jnp.float32),
            pltpu.VMEM((1, modes), jnp.float32),
        ],
        compiler_params=pltpu.CompilerParams(vmem_limit_bytes=48 * 2**20),
    )(*params, coords_now, coords_before, ref, burning, basis, basis, basis, *edges)


def layout(n, modes):
    stages, offset = [], 0
    for j in range(modes // LANES):
        needed = (j + 1) * LANES + (8 if j == RIGHT_STAGE else 0)
        size = -(-needed // (8 * n)) * 8
        stages.append((offset, size))
        offset += size * n
    return tuple(stages), offset


def sum_solve_kernel(
    n, stages, modes, part, out,
    arrived, total, work, panel_a, panel_w, plain, scaled, send_a, recv_a, send_b, recv_b,
):
    me = lax.axis_index("space")
    barrier = pltpu.get_barrier_semaphore()

    def greet(o, carry):
        pl.semaphore_signal(
            barrier, inc=1, device_id={"space": lax.rem(me + o, n)}, device_id_type=MESH
        )
        return carry

    lax.fori_loop(1, n, greet, 0)
    pl.semaphore_wait(barrier, n - 1)

    def span(stage, d):
        offset, size = stages[stage]
        return pl.ds(pl.multiple_of(offset + d * size, 8), size)

    def scatter(stage, o):
        to = lax.rem(me + o, n)
        offset, size = stages[stage]
        return pltpu.make_async_remote_copy(
            src_ref=part.at[span(stage, to)],
            dst_ref=arrived.at[o - 1, pl.ds(offset // n, size)],
            send_sem=send_a.at[stage, o - 1],
            recv_sem=recv_a.at[stage, o - 1],
            device_id={"space": to},
            device_id_type=MESH,
        )

    def gather(stage, o, owner):
        return pltpu.make_async_remote_copy(
            src_ref=total.at[span(stage, owner)],
            dst_ref=total.at[span(stage, owner)],
            send_sem=send_b.at[stage, o - 1],
            recv_sem=recv_b.at[stage, o - 1],
            device_id={"space": lax.rem(me + o, n)},
            device_id_type=MESH,
        )

    def start_sum(stage):
        def body(o, carry):
            scatter(stage, o).start()
            return carry

        lax.fori_loop(1, n, body, 0)

    def pass_on(stage):
        offset, size = stages[stage]

        def add(o, sums):
            scatter(stage, o).wait_recv()
            return sums + arrived[o - 1, offset // n : offset // n + size, :]

        def send(o, carry):
            gather(stage, o, me).start()
            return carry

        total[span(stage, me), :] = lax.fori_loop(1, n, add, part[span(stage, me), :])
        lax.fori_loop(1, n, send, 0)

    def end_sum(stage):
        def body(o, carry):
            scatter(stage, o).wait_send()
            gather(stage, o, me).wait_send()
            gather(stage, o, lax.rem(me + n - o, n)).wait_recv()
            return carry

        lax.fori_loop(1, n, body, 0)

    lane = lax.broadcasted_iota(jnp.int32, (PANEL, LANES), 1)

    def factor_panel(p, carry):
        first = pl.multiple_of(p * PANEL, PANEL)
        rows_a = work[pl.ds(first, PANEL), 0:LANES]
        rows_w = work[pl.ds(first, PANEL), LANES:]
        turned = pltpu.roll(rows_a, LANES - first, 1)
        a = [rows_a[i : i + 1, :] for i in range(PANEL)]
        w = [rows_w[i : i + 1, :] for i in range(PANEL)]
        s = {
            (i, j): jnp.broadcast_to(turned[i : i + 1, j : j + 1], (1, LANES))
            for i in range(PANEL)
            for j in range(i, PANEL)
        }
        for k in range(PANEL):
            inverse = reciprocal(s[k, k])
            for i in range(k + 1, PANEL):
                m = s[k, i] * inverse
                for j in range(i, PANEL):
                    s[i, j] = s[i, j] - m * s[k, j]
                a[i] = a[i] - m * a[k]
                w[i] = w[i] - m * w[k]
            panel_a[k : k + 1, :] = a[k] * inverse
            panel_w[k : k + 1, 0:LANES] = a[k]
            panel_w[k : k + 1, LANES:] = w[k]
            panel_w[PANEL + k : PANEL + k + 1, LANES:] = w[k] * inverse
        both = panel_w[0:PANEL, :]
        plain[pl.ds(first, PANEL), :] = both[:, LANES:]
        scaled[pl.ds(first, PANEL), :] = panel_w[PANEL:, LANES:]
        below = jnp.where(lane >= first + PANEL, panel_a[...], 0.0)
        work[...] = work[...] - tn_dot(below, both, HIGH)
        return carry

    def factor(low, high):
        lax.fori_loop(low, high, factor_panel, 0)

    def block(i, j):
        return total[stages[j][0] + i * LANES : stages[j][0] + (i + 1) * LANES, :]

    def dot(a, b):
        return jnp.dot(a, b, precision=HIGH, preferred_element_type=jnp.float32)

    count = modes // LANES
    panels = LANES // PANEL
    row = lax.broadcasted_iota(jnp.int32, (LANES, LANES), 0)
    col = lax.broadcasted_iota(jnp.int32, (LANES, LANES), 1)
    eye = jnp.where(row == col, 1.0, 0.0).astype(jnp.float32)

    between = {(0, panels // 4): [1], (0, panels * 3 // 4): [2], (1, panels // 2): [3]}
    start_sum(0)
    pass_on(0)
    start_sum(1)

    inverses, upper, forward, z, b = [], {}, {}, [], None
    for k in range(count):
        end_sum(k)
        if k + 2 < count:
            start_sum(k + 2)
        if k == RIGHT_STAGE:
            used = stages[k][0] + (k + 1) * LANES
            b = [total[used + i : used + i + 1, :] for i in range(count)]
        for i in range(k + 1):
            current = block(i, k)
            for r in range(i):
                current = current - tn_dot(upper[r, i], forward[r, k], HIGH)
            if i < k:
                upper[i, k] = current
                forward[i, k] = dot(inverses[i], current)
        work[:, 0:LANES] = current
        work[:, LANES:] = eye
        done = 0
        for at in range(1, panels):
            for stage in between.get((k, at), ()):
                factor(done, at)
                pass_on(stage)
                done = at
        factor(done, panels)
        inverses.append(tn_dot(scaled[...], plain[...], HIGH))
    for k in range(count):
        current = b[k]
        for r in range(k):
            current = current - dot(z[r], upper[r, k])
        z.append(dot(current, inverses[k]))
    x = [None] * count
    for k in reversed(range(count)):
        x[k] = z[k]
        for j in range(k + 1, count):
            x[k] = x[k] - nt_dot(x[j], forward[k, j], HIGH)
        out[:, k * LANES : (k + 1) * LANES] = -x[k]


def sum_and_solve(n, stages, modes, part):
    rows = part.shape[0]
    dma = pltpu.SemaphoreType.DMA((len(stages), n - 1))
    vmem = pl.BlockSpec(memory_space=pltpu.VMEM)
    return pl.pallas_call(
        functools.partial(sum_solve_kernel, n, stages, modes),
        out_shape=jax.ShapeDtypeStruct((1, modes), jnp.float32),
        in_specs=[vmem],
        out_specs=vmem,
        scratch_shapes=[
            pltpu.VMEM((n - 1, rows // n, LANES), jnp.float32),
            pltpu.VMEM((rows, LANES), jnp.float32),
            pltpu.VMEM((LANES, 2 * LANES), jnp.float32),
            pltpu.VMEM((PANEL, LANES), jnp.float32),
            pltpu.VMEM((2 * PANEL, 2 * LANES), jnp.float32),
            pltpu.VMEM((LANES, LANES), jnp.float32),
            pltpu.VMEM((LANES, LANES), jnp.float32),
            dma,
            dma,
            dma,
            dma,
        ],
        compiler_params=pltpu.CompilerParams(
            collective_id=1, has_side_effects=True, vmem_limit_bytes=32 * 2**20
        ),
    )(part)


def on_device(
    basis_rows,
    reference_state,
    burning,
    coords_now,
    coords_before,
    diffusivity,
    advection,
    reaction_rate,
):
    n = lax.axis_size("space")
    modes = basis_rows.shape[2]
    stages, packed_rows = layout(n, modes)
    edges = halo(n, basis_rows, reference_state)
    jacobian, residual, packed = assemble(
        stages,
        packed_rows,
        (diffusivity, advection, reaction_rate),
        coords_now,
        coords_before,
        reference_state,
        burning[None],
        basis_rows,
        edges,
    )
    update = sum_and_solve(n, stages, modes, packed)
    return (jacobian[None], residual[None], update)


def solution(mesh):
    in_specs = (
        P(None, "space", None),
        P(None, "space"),
        P("space"),
        P("inst", None),
        P("inst", None),
        P("inst"),
        P("inst"),
        P("inst"),
    )
    out_specs = (P("inst", None, "space", None), P("inst", None, "space"), P("inst", None))
    return jax.shard_map(
        on_device, mesh=mesh, in_specs=in_specs, out_specs=out_specs, check_vma=False
    )
```

```python
import functools

import jax
import jax.numpy as jnp
from jax import lax
from jax.experimental import pallas as pl
from jax.experimental.pallas import tpu as pltpu
from jax.sharding import PartitionSpec as P

time_step = 0.5
MESH = pl.DeviceIdType.MESH
TILE = 512
ROWS = 32
LANES = 128
EDGE = 16
HIGH = lax.Precision.HIGHEST
PANEL = 16
RIGHT_STAGE = 1


def tn_dot(a, b, precision=None):
    return lax.dot_general(
        a, b, (((0,), (0,)), ((), ())), preferred_element_type=jnp.float32, precision=precision
    )


def nt_dot(a, b, precision=None):
    return lax.dot_general(
        a, b, (((1,), (1,)), ((), ())), preferred_element_type=jnp.float32, precision=precision
    )


def reciprocal(x):
    guess = pl.reciprocal(x, approx=True)
    guess = guess + guess * (1.0 - x * guess)
    return guess + guess * (1.0 - x * guess)


def halo_kernel(
    n, now_ref, before_ref, ref_ref, rows, basis, ref, edge_b, state, land_b, land_r, send, recv
):
    tile, tiles = pl.program_id(0), pl.num_programs(0)
    me = lax.axis_index("space")
    cells, modes = basis.shape[1:]
    has_low, has_high = me > 0, me < n - 1
    first, last = tile == 0, tile == tiles - 1

    @pl.when(first)
    def _():
        land_b[...] = jnp.zeros_like(land_b)
        land_r[...] = jnp.zeros_like(land_r)
        state[...] = jnp.zeros_like(state)
        barrier = pltpu.get_barrier_semaphore()
        for step in (1, n - 1):
            pl.semaphore_signal(
                barrier, inc=1, device_id={"space": lax.rem(me + step, n)}, device_id_type=MESH
            )
        pl.semaphore_wait(barrier, 2)

    up = {"space": lax.rem(me + 1, n)}
    down = {"space": lax.rem(me + n - 1, n)}

    def copy(src, dst, slot, target):
        return pltpu.make_async_remote_copy(
            src_ref=src,
            dst_ref=dst,
            send_sem=send.at[slot],
            recv_sem=recv.at[slot],
            device_id=target,
            device_id_type=MESH,
        )

    to_up = [
        copy(basis.at[:, pl.ds(cells - EDGE, EDGE), :], land_b.at[0], 0, up),
        copy(ref.at[:, pl.ds(cells - LANES, LANES)], land_r.at[0], 1, up),
    ]
    to_down = [
        copy(basis.at[:, pl.ds(0, EDGE), :], land_b.at[1], 2, down),
        copy(ref.at[:, pl.ds(0, LANES)], land_r.at[1], 3, down),
    ]

    @pl.when(first & has_high)
    def _():
        for c in to_up:
            c.start()

    @pl.when(first & has_low)
    def _():
        for c in to_down:
            c.start()

    row = lax.broadcasted_iota(jnp.int32, (16, modes), 0)
    now = now_ref[...]
    vec = jnp.where(row == 0, now, jnp.where(row == 1, now - before_ref[...], 0.0))
    vec = vec.astype(jnp.bfloat16)
    here = pl.ds(pl.multiple_of(tile * TILE, TILE), TILE)
    inner = pl.ds(pl.multiple_of(tile * TILE + LANES, LANES), TILE)
    for v in range(2):
        both = nt_dot(vec, rows[v])
        state[v : v + 1, inner] = both[0:1] + ref_ref[v : v + 1, here]
        state[v + 2 : v + 3, inner] = both[1:2]

    @pl.when(last & has_high)
    def _():
        for c in to_up:
            c.wait_send()
        for c in to_down:
            c.wait_recv()

    @pl.when(last & has_low)
    def _():
        for c in to_down:
            c.wait_send()
        for c in to_up:
            c.wait_recv()

    @pl.when(last)
    def _():
        edge_b[...] = land_b[...]
        lane = lax.broadcasted_iota(jnp.int32, (1, LANES), 1)
        for v in range(2):
            low = nt_dot(vec, land_b[0, v])[0:1, EDGE - 1 : EDGE]
            state[v : v + 1, 0:LANES] = jnp.where(
                lane == LANES - 1, land_r[0, v : v + 1, :] + low, 0.0
            )
            high = nt_dot(vec, land_b[1, v])[0:1, 0:1]
            state[v : v + 1, LANES + cells : 2 * LANES + cells] = jnp.where(
                lane == 0, land_r[1, v : v + 1, :] + high, 0.0
            )


def halo(n, coords_now, coords_before, basis, ref):
    cells, modes = basis.shape[1:]

    def whole(shape):
        return pl.BlockSpec(shape, lambda i: (0,) * len(shape))

    wide = (8, cells + 2 * LANES)
    edge = (2, 2, EDGE, modes)
    return pl.pallas_call(
        functools.partial(halo_kernel, n),
        grid=(cells // TILE,),
        out_shape=[
            jax.ShapeDtypeStruct(edge, jnp.bfloat16),
            jax.ShapeDtypeStruct(wide, jnp.float32),
        ],
        in_specs=[
            whole(coords_now.shape),
            whole(coords_before.shape),
            whole(ref.shape),
            pl.BlockSpec((2, TILE, modes), lambda i: (0, i, 0)),
            pl.BlockSpec(memory_space=pl.ANY),
            pl.BlockSpec(memory_space=pl.ANY),
        ],
        out_specs=[whole(edge), whole(wide)],
        scratch_shapes=[
            pltpu.VMEM(edge, jnp.bfloat16),
            pltpu.VMEM((2, 2, LANES), jnp.float32),
            pltpu.SemaphoreType.DMA((4,)),
            pltpu.SemaphoreType.DMA((4,)),
        ],
        compiler_params=pltpu.CompilerParams(
            collective_id=0, has_side_effects=True, vmem_limit_bytes=32 * 2**20
        ),
    )(coords_now, coords_before, ref, basis, basis, ref)


def main_kernel(
    stages, diffusivity, advection, rate, burn_ref, basis, before_rows, after_rows, edge_b, state,
    jac, res_out, packed,
    coef, resid, wide, top, bottom, right,
):
    tile, tiles = pl.program_id(0), pl.num_programs(0)
    cells = res_out.shape[1]
    modes = basis.shape[2]
    half = modes // 2
    here = pl.ds(pl.multiple_of(tile * TILE, TILE), TILE)
    h = time_step
    nu, c, k = diffusivity[0], advection[0], rate[0]

    @pl.when(tile == 0)
    def _():
        resid[...] = jnp.zeros_like(resid)
        top[...] = jnp.zeros_like(top)
        bottom[...] = jnp.zeros_like(bottom)
        right[...] = jnp.zeros_like(right)
        full = state[...]
        total = full.shape[1]
        centre = full[:, LANES : LANES + cells]
        left = pltpu.roll(full, 1, 1)[:, LANES : LANES + cells]
        after = pltpu.roll(full, total - 1, 1)[:, LANES : LANES + cells]
        flux = nu * (left - 2.0 * centre + after) - c * (centre - left)
        fuel, heat = centre[0:1], centre[1:2]
        active = burn_ref[...].astype(jnp.float32)
        tangent = jnp.tanh(heat)
        slope_fuel = k * active * (1.0 + tangent)
        slope_heat = k * active * fuel * (1.0 - tangent * tangent)
        reaction = k * active * fuel * (1.0 + tangent)
        res_fuel = centre[2:3] - h * (flux[0:1] - reaction)
        res_heat = centre[3:4] - h * (flux[1:2] + reaction)
        res_out[0:1, :] = res_fuel
        res_out[1:2, :] = res_heat
        resid[0:1, :] = res_fuel
        resid[1:2, :] = res_heat
        row = lax.broadcasted_iota(jnp.int32, (8, cells), 0)
        stacked = jnp.where(row == 0, h * slope_fuel, jnp.where(row == 1, h * slope_heat, 0.0))
        for part in range(cells // LANES):
            span = slice(part * LANES, (part + 1) * LANES)
            coef[span, :] = stacked[:, span].T

    for v in range(2):
        wide[v, 8 : 8 + TILE, :] = basis[v].astype(jnp.float32)
        before = jnp.where(tile == 0, edge_b[0, v], before_rows[v]).astype(jnp.float32)
        wide[v, 0:8, :] = before[EDGE - 8 : EDGE]
        after = jnp.where(tile == tiles - 1, edge_b[1, v], after_rows[v]).astype(jnp.float32)
        wide[v, 8 + TILE : 16 + TILE, :] = after[0:8]
    base = 1.0 + 2.0 * h * nu + h * c
    to_left = -h * (nu + c)
    to_right = -h * nu

    for start in range(0, TILE, ROWS):
        at = pl.ds(pl.multiple_of(tile * TILE + start, ROWS), ROWS)
        pair = coef[at, :]
        ha, he = pair[:, 0:1], pair[:, 1:2]
        centre, side = [], []
        for v in range(2):
            centre.append(wide[v, 8 + start : 8 + start + ROWS, :])
            side.append(
                to_left * wide[v, 7 + start : 7 + start + ROWS, :]
                + to_right * wide[v, 9 + start : 9 + start + ROWS, :]
            )
        fuel_rows = (base + ha) * centre[0] + side[0] + he * centre[1]
        heat_rows = (base - he) * centre[1] + side[1] - ha * centre[0]
        jac[0, start : start + ROWS, :] = fuel_rows.astype(jnp.bfloat16)
        jac[1, start : start + ROWS, :] = heat_rows.astype(jnp.bfloat16)

    rows = jac[...].reshape(2 * TILE, modes)
    top[...] += tn_dot(rows[:, 0:half], rows)
    bottom[...] += tn_dot(rows[:, half:], rows[:, half:])
    both = resid[:, here].astype(jnp.bfloat16)
    part_fuel = jnp.dot(both, jac[0], preferred_element_type=jnp.float32)
    part_heat = jnp.dot(both, jac[1], preferred_element_type=jnp.float32)
    right[...] += part_fuel[0:1] + part_heat[1:2]

    @pl.when(tile == tiles - 1)
    def _():
        packed[...] = jnp.zeros_like(packed)
        for stage, (offset, _) in enumerate(stages):
            j = stage
            for i in range(j + 1):
                if i * LANES < half:
                    block = top[i * LANES : (i + 1) * LANES, j * LANES : (j + 1) * LANES]
                else:
                    first, second = i * LANES - half, j * LANES - half
                    block = bottom[first : first + LANES, second : second + LANES]
                packed[offset + i * LANES : offset + (i + 1) * LANES, :] = block
        used = stages[RIGHT_STAGE][0] + (RIGHT_STAGE + 1) * LANES
        for i in range(modes // LANES):
            packed[used + i : used + i + 1, :] = right[:, i * LANES : (i + 1) * LANES]


def assemble(stages, packed_rows, params, burning, basis, edge_b, state):
    cells, modes = basis.shape[1:]
    tiles = cells // TILE
    per = TILE // EDGE
    last = cells // EDGE - 1
    smem = pl.BlockSpec(memory_space=pltpu.SMEM)
    vmem = pl.BlockSpec(memory_space=pltpu.VMEM)
    half = modes // 2

    def whole(array):
        return pl.BlockSpec(array.shape, lambda i: (0,) * array.ndim)

    return pl.pallas_call(
        functools.partial(main_kernel, stages),
        grid=(tiles,),
        out_shape=[
            jax.ShapeDtypeStruct((2, cells, modes), jnp.bfloat16),
            jax.ShapeDtypeStruct((2, cells), jnp.float32),
            jax.ShapeDtypeStruct((packed_rows, LANES), jnp.float32),
        ],
        in_specs=[smem] * 3
        + [whole(burning)]
        + [
            pl.BlockSpec((2, TILE, modes), lambda i: (0, i, 0)),
            pl.BlockSpec((2, EDGE, modes), lambda i: (0, jnp.maximum(i * per - 1, 0), 0)),
            pl.BlockSpec((2, EDGE, modes), lambda i: (0, jnp.minimum((i + 1) * per, last), 0)),
        ]
        + [whole(edge_b), whole(state)],
        out_specs=[
            pl.BlockSpec((2, TILE, modes), lambda i: (0, i, 0)),
            vmem,
            vmem,
        ],
        scratch_shapes=[
            pltpu.VMEM((cells, 8), jnp.float32),
            pltpu.VMEM((16, cells), jnp.float32),
            pltpu.VMEM((2, TILE + 16, modes), jnp.float32),
            pltpu.VMEM((half, modes), jnp.float32),
            pltpu.VMEM((half, half), jnp.float32),
            pltpu.VMEM((1, modes), jnp.float32),
        ],
        compiler_params=pltpu.CompilerParams(vmem_limit_bytes=48 * 2**20),
    )(*params, burning, basis, basis, basis, edge_b, state)


def layout(n, modes):
    stages, offset = [], 0
    for j in range(modes // LANES):
        needed = (j + 1) * LANES + (8 if j == RIGHT_STAGE else 0)
        size = -(-needed // (8 * n)) * 8
        stages.append((offset, size))
        offset += size * n
    return tuple(stages), offset


def sum_solve_kernel(
    n, stages, modes, part, out,
    arrived, total, work, panel_a, panel_w, plain, scaled, send_a, recv_a, send_b, recv_b,
):
    me = lax.axis_index("space")
    barrier = pltpu.get_barrier_semaphore()

    def greet(o, carry):
        pl.semaphore_signal(
            barrier, inc=1, device_id={"space": lax.rem(me + o, n)}, device_id_type=MESH
        )
        return carry

    lax.fori_loop(1, n, greet, 0)
    pl.semaphore_wait(barrier, n - 1)

    def span(stage, d):
        offset, size = stages[stage]
        return pl.ds(pl.multiple_of(offset + d * size, 8), size)

    def scatter(stage, o):
        to = lax.rem(me + o, n)
        offset, size = stages[stage]
        return pltpu.make_async_remote_copy(
            src_ref=part.at[span(stage, to)],
            dst_ref=arrived.at[o - 1, pl.ds(offset // n, size)],
            send_sem=send_a.at[stage, o - 1],
            recv_sem=recv_a.at[stage, o - 1],
            device_id={"space": to},
            device_id_type=MESH,
        )

    def gather(stage, o, owner):
        return pltpu.make_async_remote_copy(
            src_ref=total.at[span(stage, owner)],
            dst_ref=total.at[span(stage, owner)],
            send_sem=send_b.at[stage, o - 1],
            recv_sem=recv_b.at[stage, o - 1],
            device_id={"space": lax.rem(me + o, n)},
            device_id_type=MESH,
        )

    def start_sum(stage):
        def body(o, carry):
            scatter(stage, o).start()
            return carry

        lax.fori_loop(1, n, body, 0)

    def pass_on(stage):
        offset, size = stages[stage]

        def add(o, sums):
            scatter(stage, o).wait_recv()
            return sums + arrived[o - 1, offset // n : offset // n + size, :]

        def send(o, carry):
            gather(stage, o, me).start()
            return carry

        total[span(stage, me), :] = lax.fori_loop(1, n, add, part[span(stage, me), :])
        lax.fori_loop(1, n, send, 0)

    def end_sum(stage):
        def body(o, carry):
            scatter(stage, o).wait_send()
            gather(stage, o, me).wait_send()
            gather(stage, o, lax.rem(me + n - o, n)).wait_recv()
            return carry

        lax.fori_loop(1, n, body, 0)

    lane = lax.broadcasted_iota(jnp.int32, (PANEL, LANES), 1)

    def factor_panel(p, carry):
        first = pl.multiple_of(p * PANEL, PANEL)
        rows_a = work[pl.ds(first, PANEL), 0:LANES]
        rows_w = work[pl.ds(first, PANEL), LANES:]
        turned = pltpu.roll(rows_a, LANES - first, 1)
        a = [rows_a[i : i + 1, :] for i in range(PANEL)]
        w = [rows_w[i : i + 1, :] for i in range(PANEL)]
        s = {
            (i, j): jnp.broadcast_to(turned[i : i + 1, j : j + 1], (1, LANES))
            for i in range(PANEL)
            for j in range(i, PANEL)
        }
        for k in range(PANEL):
            inverse = reciprocal(s[k, k])
            for i in range(k + 1, PANEL):
                m = s[k, i] * inverse
                for j in range(i, PANEL):
                    s[i, j] = s[i, j] - m * s[k, j]
                a[i] = a[i] - m * a[k]
                w[i] = w[i] - m * w[k]
            panel_a[k : k + 1, :] = a[k] * inverse
            panel_w[k : k + 1, 0:LANES] = a[k]
            panel_w[k : k + 1, LANES:] = w[k]
            panel_w[PANEL + k : PANEL + k + 1, LANES:] = w[k] * inverse
        both = panel_w[0:PANEL, :]
        plain[pl.ds(first, PANEL), :] = both[:, LANES:]
        scaled[pl.ds(first, PANEL), :] = panel_w[PANEL:, LANES:]
        below = jnp.where(lane >= first + PANEL, panel_a[...], 0.0)
        work[...] = work[...] - tn_dot(below, both, HIGH)
        return carry

    def factor(low, high):
        lax.fori_loop(low, high, factor_panel, 0)

    def block(i, j):
        return total[stages[j][0] + i * LANES : stages[j][0] + (i + 1) * LANES, :]

    def dot(a, b):
        return jnp.dot(a, b, precision=HIGH, preferred_element_type=jnp.float32)

    count = modes // LANES
    panels = LANES // PANEL
    row = lax.broadcasted_iota(jnp.int32, (LANES, LANES), 0)
    col = lax.broadcasted_iota(jnp.int32, (LANES, LANES), 1)
    eye = jnp.where(row == col, 1.0, 0.0).astype(jnp.float32)

    between = {(0, panels // 4): [1], (0, panels * 3 // 4): [2], (1, panels // 2): [3]}
    start_sum(0)
    pass_on(0)
    start_sum(1)

    inverses, upper, forward, z, b = [], {}, {}, [], None
    for k in range(count):
        end_sum(k)
        if k + 2 < count:
            start_sum(k + 2)
        if k == RIGHT_STAGE:
            used = stages[k][0] + (k + 1) * LANES
            b = [total[used + i : used + i + 1, :] for i in range(count)]
        for i in range(k + 1):
            current = block(i, k)
            for r in range(i):
                current = current - tn_dot(upper[r, i], forward[r, k], HIGH)
            if i < k:
                upper[i, k] = current
                forward[i, k] = dot(inverses[i], current)
        work[:, 0:LANES] = current
        work[:, LANES:] = eye
        done = 0
        for at in range(1, panels):
            for stage in between.get((k, at), ()):
                factor(done, at)
                pass_on(stage)
                done = at
        factor(done, panels)
        inverses.append(tn_dot(scaled[...], plain[...], HIGH))
    for k in range(count):
        current = b[k]
        for r in range(k):
            current = current - dot(z[r], upper[r, k])
        z.append(dot(current, inverses[k]))
    x = [None] * count
    for k in reversed(range(count)):
        x[k] = z[k]
        for j in range(k + 1, count):
            x[k] = x[k] - nt_dot(x[j], forward[k, j], HIGH)
        out[:, k * LANES : (k + 1) * LANES] = -x[k]


def sum_and_solve(n, stages, modes, part):
    rows = part.shape[0]
    dma = pltpu.SemaphoreType.DMA((len(stages), n - 1))
    vmem = pl.BlockSpec(memory_space=pltpu.VMEM)
    return pl.pallas_call(
        functools.partial(sum_solve_kernel, n, stages, modes),
        out_shape=jax.ShapeDtypeStruct((1, modes), jnp.float32),
        in_specs=[vmem],
        out_specs=vmem,
        scratch_shapes=[
            pltpu.VMEM((n - 1, rows // n, LANES), jnp.float32),
            pltpu.VMEM((rows, LANES), jnp.float32),
            pltpu.VMEM((LANES, 2 * LANES), jnp.float32),
            pltpu.VMEM((PANEL, LANES), jnp.float32),
            pltpu.VMEM((2 * PANEL, 2 * LANES), jnp.float32),
            pltpu.VMEM((LANES, LANES), jnp.float32),
            pltpu.VMEM((LANES, LANES), jnp.float32),
            dma,
            dma,
            dma,
            dma,
        ],
        compiler_params=pltpu.CompilerParams(
            collective_id=1, has_side_effects=True, vmem_limit_bytes=32 * 2**20
        ),
    )(part)


def on_device(
    basis_rows,
    reference_state,
    burning,
    coords_now,
    coords_before,
    diffusivity,
    advection,
    reaction_rate,
):
    n = lax.axis_size("space")
    modes = basis_rows.shape[2]
    stages, packed_rows = layout(n, modes)
    edge_b, state = halo(n, coords_now, coords_before, basis_rows, reference_state)
    jacobian, residual, packed = assemble(
        stages,
        packed_rows,
        (diffusivity, advection, reaction_rate),
        burning[None],
        basis_rows,
        edge_b,
        state,
    )
    update = sum_and_solve(n, stages, modes, packed)
    return (jacobian[None], residual[None], update)


def solution(mesh):
    in_specs = (
        P(None, "space", None),
        P(None, "space"),
        P("space"),
        P("inst", None),
        P("inst", None),
        P("inst"),
        P("inst"),
        P("inst"),
    )
    out_specs = (P("inst", None, "space", None), P("inst", None, "space"), P("inst", None))
    return jax.shard_map(
        on_device, mesh=mesh, in_specs=in_specs, out_specs=out_specs, check_vma=False
    )
```
